32 devices in a mesh: row: 4 (over z), col: 8 (over y, x, core).
Axes of the slice: x: 2, y: 2, z: 4, core: 2. Of those that a mesh axis runs over, the one named last changes fastest.
Arguments:
- user_factors: float32 [4096, 128], P(('col', 'row')), may hold values from -16 to 16
- item_factors: bfloat16 [65536, 128], P(('row', 'col')), may hold values from -0.046875 to 0.046875
- confidence: bfloat16 [4, 8, 32768, 128], P('row', 'col'), may hold values from 0 to 40, as said below
- tile_coords: int32 [4, 8, 256, 2], P('row', 'col'), may hold values from 0 to 127, as said below
- relay_source: int32 [8, 4], P('col', 'row'), may hold values from 0 to 3, each once within a row
Outputs:
- solved: float32 [4096, 128], P(('col', 'row'))
- residual: float32 [4096, 128], P(('col', 'row'))
The draws below stay inside these ranges and needn't reach their ends.
Inputs may be any that keep to these rules, and one draw needn't show every extreme that they name: `confidence`: zero where an entry is not observed, else between 1 and 40. `tile_coords`: within one device no (user block, item block) pair repeats; column 0 is below 4, column 1 below 128.
All inputs are finite; a program needn't handle non-finite values.
Results may differ from the reference program's by a relative error of at most 0.03.
The reference program's roundings to bfloat16 on the way count: a program that leaves them out, or rounds other values in their place, can miss the bound.
Values may be sent and summed in bfloat16 or wider, within the bound.
A program may use at most 128 MiB of HBM per device.

```python
import math
import jax
import jax.numpy as jnp
from jax import lax

K = 128
BLK = 128
ITERS = 3
NT_DEV = 256
UBG = 4
IBG = 128
USERS = 4096
ITEMS = 65536
N_ROW = 4
N_COL = 8


def choose_tiles(device_key):
    return jax.random.permutation(device_key, UBG * IBG)[:NT_DEV]


def tile_layout(key):
    device_keys = jax.random.split(jax.random.fold_in(key, 21), N_ROW * N_COL)
    chosen = jax.vmap(choose_tiles)(device_keys).astype(jnp.int32)
    stacked = jnp.stack([chosen // IBG, chosen % IBG], axis=-1)
    return stacked.reshape(N_ROW, N_COL, NT_DEV, 2).astype(jnp.int32)


def log_range(key, extent, lowest, highest):
    return jnp.exp(jax.random.uniform(key, extent, jnp.float32, math.log(lowest), math.log(highest)))


def draw_confidence(key, part):
    coords = tile_layout(key)
    density = log_range(jax.random.fold_in(key, 31), (N_ROW, N_COL, NT_DEV), 0.02, 0.9)
    activity = log_range(jax.random.fold_in(key, 32), (N_COL, UBG, BLK), 0.1, 4.0)
    appeal = log_range(jax.random.fold_in(key, 33), (N_ROW, IBG, BLK), 0.3, 3.0)
    col_index = jnp.arange(N_COL, dtype=jnp.int32)[None, :, None]
    row_index = jnp.arange(N_ROW, dtype=jnp.int32)[:, None, None]
    user_rate = activity[col_index, coords[..., 0]]
    item_rate = appeal[row_index, coords[..., 1]]
    chance = jnp.minimum(density[..., None, None] * user_rate[..., :, None] * item_rate[..., None, :], 0.95)
    observed = jax.random.uniform(jax.random.fold_in(key, 11), chance.shape, jnp.float32) < chance
    strength = log_range(jax.random.fold_in(key, 12), chance.shape, 1.0, 40.0)
    values = jnp.where(observed, strength, 0.0)
    return values.reshape(N_ROW, N_COL, NT_DEV * BLK, BLK).astype(jnp.bfloat16)


def draw_tile_coords(key, part):
    return tile_layout(key)


def block_scale(stream_key, shape, cuts, low, high):
    gain = 1.0
    for dim, shards_of in cuts:
        draws = jax.random.uniform(jax.random.fold_in(jax.random.fold_in(stream_key, 6), dim), (shards_of,), jnp.float32, low / len(cuts), high / len(cuts))
        gain = gain * jnp.repeat(jnp.exp(draws), shape[dim] // shards_of).reshape((-1,) + (1,) * (len(shape) - 1 - dim))
    return gain


def scatter_about(key, shape, scale, limit, cuts=(), held_as=jnp.bfloat16):
    array = scale * jax.random.normal(key, shape, jnp.float32)
    if cuts:
        array = array * block_scale(key, shape, cuts, -0.22, 0.18)
    return jnp.clip(array, -limit, limit).astype(held_as)


def setup_inputs(seed: int = 0) -> dict:
    keys = jax.random.split(jax.random.key(seed), 6)
    return {
        "user_factors": scatter_about(keys[0], (USERS, K), 3.0, 16.0, ((0, 32),), jnp.float32),
        "item_factors": scatter_about(keys[1], (ITEMS, K), (ITEMS // 4) ** -0.5, 0.046875, ((0, 32),)),
        "confidence": draw_confidence(jax.random.fold_in(keys[5], 71), 0),
        "tile_coords": draw_tile_coords(jax.random.fold_in(keys[5], 71), 0),
        "relay_source": jax.vmap(lambda own: jax.random.permutation(own, UBG))(jax.random.split(keys[4], N_COL)).reshape((N_COL, UBG)).astype(jnp.int32),
    }


ridge = 0.1
epsilon = 1e-6


def device_terms(index, source, item_factors, confidence, tile_coords, use_targets):
    row_index = index // N_COL
    col_index = index % N_COL
    coords = tile_coords[row_index, col_index]
    weights = confidence[row_index, col_index].reshape(NT_DEV, BLK, BLK).astype(jnp.float32)
    item_group = lax.dynamic_slice_in_dim(item_factors, (row_index * IBG * BLK).astype(jnp.int32), IBG * BLK, 0).reshape(IBG, BLK, K)
    item_tiles = item_group[coords[:, 1]].astype(jnp.float32)
    if use_targets:
        values = jnp.where(weights > 0, weights + 1.0, 0.0).astype(jnp.bfloat16)
    else:
        user_group = lax.dynamic_slice_in_dim(source, (col_index * UBG * BLK).astype(jnp.int32), UBG * BLK, 0).reshape(UBG, BLK, K)
        picked = user_group[coords[:, 0]].astype(jnp.float32)
        scores = jnp.einsum("tuk,tik->tui", picked, item_tiles)
        values = (scores * weights).astype(jnp.bfloat16)
    values = lax.optimization_barrier(values).astype(jnp.float32)
    terms = jnp.einsum("tui,tik->tuk", values, item_tiles)
    summed = jax.ops.segment_sum(terms, coords[:, 0], num_segments=UBG)
    return summed.reshape(UBG * BLK, K), col_index


def tile_total(source, item_factors, confidence, tile_coords, use_targets):
    def visit(total, index):
        part, col_index = device_terms(index, source, item_factors, confidence, tile_coords, use_targets)
        start = (col_index * UBG * BLK).astype(jnp.int32)
        before = lax.dynamic_slice_in_dim(total, start, UBG * BLK, 0)
        return lax.dynamic_update_slice_in_dim(total, before + part, start, 0), None

    empty = jnp.zeros((USERS, K), jnp.float32)
    total, unused = lax.scan(visit, empty, jnp.arange(N_ROW * N_COL, dtype=jnp.int32))
    return total


def reference(user_factors, item_factors, confidence, tile_coords, relay_source):
    gram_matrix = jnp.dot(item_factors.T, item_factors, preferred_element_type=jnp.float32)

    def operate(vector):
        rounded = vector.astype(jnp.bfloat16)
        local = jnp.dot(vector, gram_matrix, precision=lax.Precision.HIGHEST) + ridge * vector
        return local + tile_total(rounded, item_factors, confidence, tile_coords, False)

    right_side = tile_total(user_factors.astype(jnp.bfloat16), item_factors, confidence, tile_coords, True)
    solution = user_factors
    residual = right_side - operate(solution)
    direction = residual
    norm_now = jnp.sum(residual * residual, axis=1, keepdims=True)
    for iteration in range(ITERS):
        image = operate(direction)
        step_size = norm_now / (jnp.sum(direction * image, axis=1, keepdims=True) + epsilon)
        solution = solution + step_size * direction
        residual = residual - step_size * image
        norm_next = jnp.sum(residual * residual, axis=1, keepdims=True)
        direction = residual + (norm_next / (norm_now + epsilon)) * direction
        norm_now = norm_next
    blocks = solution.reshape(N_COL, UBG, BLK, K)
    solved = jnp.take_along_axis(blocks, relay_source[:, :, None, None], axis=1).reshape(USERS, K)
    return solved, residual
```

```python
import functools

import jax
import jax.numpy as jnp
from jax import lax
from jax.experimental import pallas as pl
from jax.experimental.pallas import tpu as pltpu
from jax.sharding import PartitionSpec as P

ITERS = 3
RIDGE = 0.1
EPSILON = 1e-06
HALVES = 2
WIDE = 4


def flip(index, mask):
    bit = 1
    while bit <= mask:
        if mask & bit:
            index = index + bit * (1 - 2 * ((index // bit) % 2))
        bit *= 2
    return index


def route(offset, half):
    if offset % 2:
        return 1
    bits = [1 << i for i in range(offset.bit_length()) if offset >> i & 1]
    if len(bits) == 2:
        return bits[1 - half]
    return offset


def kernel(
    n_row, n_col, size,
    where_ref, slot_ref, user_ref, item_ref, conf_ref,
    solved_ref, resid_ref,
    weights, items, start_users, users, part, inbox, gram, gram_in, steps, direction,
    conf_sem, item_sem, gather_send, gather_recv, row_send, row_recv,
):
    row = lax.axis_index("row")
    col = lax.axis_index("col")
    shard = item_ref.shape[0]
    half_rows = shard // HALVES
    item_blocks = items.shape[0] // size
    own_blocks = shard // size
    user_blocks = n_row
    own = pl.ds(pl.multiple_of(row * size, size), size)

    def shard_rows(mask, half):
        start = flip(col, mask) * shard + half * half_rows
        return pl.ds(pl.multiple_of(start, size), half_rows)

    def gather_copy(offset, half):
        delta = route(offset, half)
        held = delta ^ offset
        there = shard_rows(held, half)
        source = items.at[there] if held else item_ref.at[pl.ds(half * half_rows, half_rows)]
        return pltpu.make_async_remote_copy(
            src_ref=source,
            dst_ref=items.at[there],
            send_sem=gather_send.at[offset, half],
            recv_sem=gather_recv.at[offset, half],
            device_id=(row, flip(col, delta)),
            device_id_type=pl.DeviceIdType.MESH,
        )

    def peer(d):
        return (row + d) % n_row

    def row_copy(kind, d, source, target):
        return pltpu.make_async_remote_copy(
            src_ref=source,
            dst_ref=target,
            send_sem=row_send.at[kind, d],
            recv_sem=row_recv.at[kind, d],
            device_id=(peer(d), col),
            device_id_type=pl.DeviceIdType.MESH,
        )

    def start_copy(d):
        return row_copy(0, d, user_ref, start_users.at[row])

    def gram_copy(d):
        return row_copy(1, d, gram, gram_in.at[d - 1])

    def sum_copy(phase, d):
        block = pl.ds(pl.multiple_of(peer(d) * size, size), size)
        return row_copy(2 + phase, d, part.at[phase, block], inbox.at[phase, d - 1])

    def users_copy(step, d):
        return row_copy(3 + ITERS + step, d, users.at[step + 1, row], users.at[step + 1, row])

    def steps_copy(step, d):
        return row_copy(3 + 2 * ITERS + step, d, steps.at[step, row], steps.at[step, row])

    peers = range(1, n_row)
    loaded = pltpu.make_async_copy(conf_ref, weights.at[pl.ds(0, conf_ref.shape[0])], conf_sem)
    loaded.start()
    own_items = pltpu.make_async_copy(
        item_ref, items.at[pl.ds(pl.multiple_of(col * shard, size), shard)], item_sem
    )
    own_items.start()

    deltas = sorted({route(m, h) for m in range(1, n_col) for h in range(HALVES)})
    barrier = pltpu.get_barrier_semaphore()
    for d in peers:
        pl.semaphore_signal(
            barrier, inc=1, device_id=(peer(d), col), device_id_type=pl.DeviceIdType.MESH
        )
    for delta in deltas:
        pl.semaphore_signal(
            barrier, inc=1, device_id=(row, flip(col, delta)), device_id_type=pl.DeviceIdType.MESH
        )
    pl.semaphore_wait(barrier, n_row - 1 + len(deltas))

    pending = [(m, h) for m in range(1, n_col) for h in range(HALVES)]
    begun = []
    arrived = set()

    def send_ready(offset, half):
        for m, h in pending:
            if h == half and (route(m, h) ^ m) == offset and (m, h) not in begun:
                gather_copy(m, h).start()
                begun.append((m, h))

    def receive(offset, half):
        if (offset, half) not in arrived:
            gather_copy(offset, half).wait_recv()
            arrived.add((offset, half))
            send_ready(offset, half)

    for d in peers:
        start_copy(d).start()
    direct = [m for m in range(1, n_col) if all(route(m, h) == m for h in range(HALVES))]
    singles = [m for m in direct if m != 1]
    for turn in range(HALVES):
        for place, m in enumerate(singles):
            half = (turn + place) % HALVES
            gather_copy(m, half).start()
            begun.append((m, half))
        if turn == 0:
            for half in range(HALVES):
                gather_copy(1, half).start()
                begun.append((1, half))

    weights[conf_ref.shape[0]] = jnp.zeros((size, size), weights.dtype)
    start_users[row] = user_ref[...]
    part[...] = jnp.zeros_like(part)
    gram[...] = jnp.zeros_like(gram)
    loaded.wait()
    own_items.wait()
    for d in peers:
        start_copy(d).wait_recv()
    users[0] = start_users[...].astype(jnp.bfloat16)

    def weight_tile(block, item_block):
        tile = where_ref[block * item_blocks + item_block]
        return weights[tile]

    def terms(phase, first_block):
        rows = pl.ds(pl.multiple_of(first_block * size, size), WIDE * size)
        factors = items[rows, :]
        for block in range(user_blocks):
            mine = pl.ds(block * size, size)
            scores = lax.dot_general(
                users[phase, block], factors, (((1,), (1,)), ((), ())),
                preferred_element_type=jnp.float32,
            )
            w = jnp.concatenate(
                [weight_tile(block, first_block + i) for i in range(WIDE)], axis=1
            ).astype(jnp.float32)
            weighted = (scores * w).astype(jnp.bfloat16)
            total = jnp.dot(weighted, factors, preferred_element_type=jnp.float32)
            if phase == 0:
                targets = jnp.where(w > 0, w + 1.0, 0.0).astype(jnp.bfloat16)
                total = jnp.dot(targets, factors, preferred_element_type=jnp.float32) - total
            part[phase, mine, :] += total
        if phase == 0:
            gram[...] += lax.dot_general(
                factors, factors, (((0,), (0,)), ((), ())), preferred_element_type=jnp.float32
            )

    def first_pass(offset):
        base = flip(col, offset) * own_blocks

        def body(i, carry):
            terms(0, base + i * WIDE)
            return carry

        lax.fori_loop(0, own_blocks // WIDE, body, 0)

    evens = [m for m in range(2, n_col, 2)]
    early = [m for m in evens if m in singles]
    late = [m for m in evens if m not in singles]
    first_pass(0)
    for place, m in enumerate(early):
        receive(m, place % HALVES)
    for half in range(HALVES):
        receive(1, half)
    first_pass(1)
    for place, m in enumerate(early):
        receive(m, (place + 1) % HALVES)
    for m in early:
        first_pass(m)
    for m in late:
        for half in range(HALVES):
            receive(m, half)
    for m in early:
        for half in range(HALVES):
            receive(m + 1, half)
        first_pass(m + 1)
    for m in late:
        first_pass(m)
    for m in late:
        for half in range(HALVES):
            receive(m + 1, half)
        first_pass(m + 1)

    part[0] -= jnp.dot(
        start_users[...].reshape(part.shape[1:]), gram[...], precision=lax.Precision.HIGHEST,
        preferred_element_type=jnp.float32,
    )
    for d in peers:
        sum_copy(0, d).start()
    for d in peers:
        gram_copy(d).start()
    residual = part[0, own, :] - RIDGE * user_ref[...]
    for d in peers:
        sum_copy(0, d).wait_recv()
    for d in peers:
        residual += inbox[0, d - 1]
    resid_ref[...] = residual
    direction[...] = residual
    norm_now = jnp.sum(residual * residual, axis=1, keepdims=True)

    for step in range(ITERS):
        users[step + 1, row] = direction[...].astype(jnp.bfloat16)
        for d in peers:
            users_copy(step, d).start()
        for d in peers:
            users_copy(step, d).wait_recv()

        def body(i, carry, phase=step + 1):
            terms(phase, i * WIDE)
            return carry

        lax.fori_loop(0, item_blocks // WIDE, body, 0)
        for d in peers:
            sum_copy(step + 1, d).start()
        if step == 0:
            for d in peers:
                gram_copy(d).wait()
            whole = gram[...]
            for d in peers:
                whole += gram_in[d - 1]
            gram[...] = whole
        vector = direction[...]
        image = (
            jnp.dot(
                vector, gram[...], precision=lax.Precision.HIGHEST,
                preferred_element_type=jnp.float32,
            )
            + RIDGE * vector
            + part[step + 1, own, :]
        )
        for d in peers:
            sum_copy(step + 1, d).wait_recv()
        for d in peers:
            image += inbox[step + 1, d - 1]
        step_size = norm_now / (jnp.sum(vector * image, axis=1, keepdims=True) + EPSILON)
        spread = jnp.broadcast_to(step_size, (size, size))
        steps[step, row] = spread.T[:8]
        for d in peers:
            steps_copy(step, d).start()
        residual = resid_ref[...] - step_size * image
        resid_ref[...] = residual
        norm_next = jnp.sum(residual * residual, axis=1, keepdims=True)
        direction[...] = residual + norm_next / (norm_now + EPSILON) * vector
        norm_now = norm_next

    for step in range(ITERS):
        for d in peers:
            steps_copy(step, d).wait_recv()
    source = slot_ref[0, 0]
    answer = start_users[source]
    for step in range(ITERS):
        scale = jnp.broadcast_to(steps[step, source][0:1], (size, size)).T
        answer += scale * users[step + 1, source].astype(jnp.float32)
    solved_ref[...] = answer

    for m, h in pending:
        gather_copy(m, h).wait_send()
    for d in peers:
        start_copy(d).wait_send()
        for phase in range(ITERS + 1):
            sum_copy(phase, d).wait_send()
        for step in range(ITERS):
            users_copy(step, d).wait_send()
            steps_copy(step, d).wait_send()


def local(n_row, n_col, user_factors, item_factors, confidence, tile_coords, relay_source):
    size = confidence.shape[-1]
    width = item_factors.shape[1]
    tiles = tile_coords.shape[2]
    group_items = item_factors.shape[0] * n_col
    item_blocks = group_items // size
    group_users = user_factors.shape[0] * n_row
    coords = tile_coords[0, 0]
    key = coords[:, 0] * item_blocks + coords[:, 1]
    places = jnp.arange(n_row * item_blocks, dtype=jnp.int32)
    number = jnp.arange(tiles, dtype=jnp.int32)
    where = jnp.min(
        jnp.where(key[None, :] == places[:, None], number[None, :], tiles), axis=1
    ).astype(jnp.int32)
    kinds = 3 + 3 * ITERS
    vmem = pl.BlockSpec(memory_space=pltpu.VMEM)
    smem = pl.BlockSpec(memory_space=pltpu.SMEM)
    outs = jax.ShapeDtypeStruct(user_factors.shape, jnp.float32)
    return pl.pallas_call(
        functools.partial(kernel, n_row, n_col, size),
        out_shape=(outs, outs),
        in_specs=[smem, smem, vmem, vmem, pl.BlockSpec(memory_space=pl.ANY)],
        out_specs=(vmem, vmem),
        scratch_shapes=[
            pltpu.VMEM((tiles + 1, size, size), jnp.bfloat16),
            pltpu.VMEM((group_items, width), jnp.bfloat16),
            pltpu.VMEM((n_row, size, width), jnp.float32),
            pltpu.VMEM((ITERS + 1, n_row, size, width), jnp.bfloat16),
            pltpu.VMEM((ITERS + 1, group_users, width), jnp.float32),
            pltpu.VMEM((ITERS + 1, n_row - 1, size, width), jnp.float32),
            pltpu.VMEM((width, width), jnp.float32),
            pltpu.VMEM((n_row - 1, width, width), jnp.float32),
            pltpu.VMEM((ITERS, n_row, 8, size), jnp.float32),
            pltpu.VMEM((size, width), jnp.float32),
            pltpu.SemaphoreType.DMA,
            pltpu.SemaphoreType.DMA,
            pltpu.SemaphoreType.DMA((n_col, HALVES)),
            pltpu.SemaphoreType.DMA((n_col, HALVES)),
            pltpu.SemaphoreType.DMA((kinds, n_row)),
            pltpu.SemaphoreType.DMA((kinds, n_row)),
        ],
        compiler_params=pltpu.CompilerParams(
            collective_id=0, has_side_effects=True, vmem_limit_bytes=48 * 2**20
        ),
    )(where, relay_source, user_factors, item_factors, confidence.reshape(tiles, size, size))


def solution(mesh):
    return jax.shard_map(
        functools.partial(local, mesh.shape["row"], mesh.shape["col"]),
        mesh=mesh,
        in_specs=(
            P(("col", "row"), None),
            P(("row", "col"), None),
            P("row", "col", None, None),
            P("row", "col", None, None),
            P("col", "row"),
        ),
        out_specs=(P(("col", "row"), None), P(("col", "row"), None)),
        check_vma=False,
    )
```

```python
import functools

import jax
import jax.numpy as jnp
from jax import lax
from jax.experimental import pallas as pl
from jax.experimental.pallas import tpu as pltpu
from jax.sharding import PartitionSpec as P

ITERS = 3
RIDGE = 0.1
EPSILON = 1e-06
HALVES = 2
WIDE = 4


def flip(index, mask):
    bit = 1
    while bit <= mask:
        if mask & bit:
            index = index + bit * (1 - 2 * ((index // bit) % 2))
        bit *= 2
    return index


def route(offset, half):
    if offset % 2:
        return 1
    bits = [1 << i for i in range(offset.bit_length()) if offset >> i & 1]
    if len(bits) == 2:
        return bits[1 - half]
    return offset


def kernel(
    n_row, n_col, size,
    where_ref, slot_ref, user_ref, item_ref, conf_ref,
    solved_ref, resid_ref,
    weights, items, start_users, users, part, inbox, gram, gram_in, steps, direction,
    conf_sem, item_sem, gather_send, gather_recv, row_send, row_recv,
):
    row = lax.axis_index("row")
    col = lax.axis_index("col")
    shard = item_ref.shape[0]
    half_rows = shard // HALVES
    item_blocks = items.shape[0] // size
    own_blocks = shard // size
    user_blocks = n_row
    own = pl.ds(pl.multiple_of(row * size, size), size)

    def shard_rows(mask, half):
        start = flip(col, mask) * shard + half * half_rows
        return pl.ds(pl.multiple_of(start, size), half_rows)

    def gather_copy(offset, half):
        delta = route(offset, half)
        held = delta ^ offset
        there = shard_rows(held, half)
        source = items.at[there] if held else item_ref.at[pl.ds(half * half_rows, half_rows)]
        return pltpu.make_async_remote_copy(
            src_ref=source,
            dst_ref=items.at[there],
            send_sem=gather_send.at[offset, half],
            recv_sem=gather_recv.at[offset, half],
            device_id=(row, flip(col, delta)),
            device_id_type=pl.DeviceIdType.MESH,
        )

    def peer(d):
        return (row + d) % n_row

    def row_copy(kind, d, source, target):
        return pltpu.make_async_remote_copy(
            src_ref=source,
            dst_ref=target,
            send_sem=row_send.at[kind, d],
            recv_sem=row_recv.at[kind, d],
            device_id=(peer(d), col),
            device_id_type=pl.DeviceIdType.MESH,
        )

    def start_copy(d):
        return row_copy(0, d, user_ref, start_users.at[row])

    def gram_copy(d):
        return row_copy(1, d, gram, gram_in.at[d - 1])

    def sum_copy(phase, d):
        block = pl.ds(pl.multiple_of(peer(d) * size, size), size)
        return row_copy(2 + phase, d, part.at[phase, block], inbox.at[phase, d - 1])

    def users_copy(step, d):
        return row_copy(3 + ITERS + step, d, users.at[step + 1, row], users.at[step + 1, row])

    def steps_copy(step, d):
        return row_copy(3 + 2 * ITERS + step, d, steps.at[step, row], steps.at[step, row])

    peers = range(1, n_row)
    loaded = pltpu.make_async_copy(conf_ref, weights.at[pl.ds(0, conf_ref.shape[0])], conf_sem)
    loaded.start()
    own_items = pltpu.make_async_copy(
        item_ref, items.at[pl.ds(pl.multiple_of(col * shard, size), shard)], item_sem
    )
    own_items.start()

    deltas = sorted({route(m, h) for m in range(1, n_col) for h in range(HALVES)})
    barrier = pltpu.get_barrier_semaphore()
    for d in peers:
        pl.semaphore_signal(
            barrier, inc=1, device_id=(peer(d), col), device_id_type=pl.DeviceIdType.MESH
        )
    for delta in deltas:
        pl.semaphore_signal(
            barrier, inc=1, device_id=(row, flip(col, delta)), device_id_type=pl.DeviceIdType.MESH
        )
    pl.semaphore_wait(barrier, n_row - 1 + len(deltas))

    pending = [(m, h) for m in range(1, n_col) for h in range(HALVES)]
    begun = []
    arrived = set()

    def send_ready(offset, half):
        for m, h in pending:
            if h == half and (route(m, h) ^ m) == offset and (m, h) not in begun:
                gather_copy(m, h).start()
                begun.append((m, h))

    def receive(offset, half):
        if (offset, half) not in arrived:
            gather_copy(offset, half).wait_recv()
            arrived.add((offset, half))
            send_ready(offset, half)

    for d in peers:
        start_copy(d).start()
    direct = [m for m in range(1, n_col) if all(route(m, h) == m for h in range(HALVES))]
    singles = [m for m in direct if m != 1]
    for turn in range(HALVES):
        for place, m in enumerate(singles):
            half = (turn + place) % HALVES
            gather_copy(m, half).start()
            begun.append((m, half))
        if turn == 0:
            for half in range(HALVES):
                gather_copy(1, half).start()
                begun.append((1, half))

    weights[conf_ref.shape[0]] = jnp.zeros((size, size), weights.dtype)
    start_users[row] = user_ref[...]
    part[...] = jnp.zeros_like(part)
    gram[...] = jnp.zeros_like(gram)
    loaded.wait()
    own_items.wait()
    for d in peers:
        start_copy(d).wait_recv()
    users[0] = start_users[...].astype(jnp.bfloat16)

    def weight_tile(block, item_block):
        tile = where_ref[block * item_blocks + item_block]
        return weights[tile]

    def terms(phase, first_block):
        rows = pl.ds(pl.multiple_of(first_block * size, size), WIDE * size)
        factors = items[rows, :]
        scores = lax.dot_general(
            users[phase].reshape(part.shape[1:]), factors, (((1,), (1,)), ((), ())),
            preferred_element_type=jnp.float32,
        )
        w = jnp.concatenate(
            [
                jnp.concatenate(
                    [weight_tile(block, first_block + i) for i in range(WIDE)], axis=1
                )
                for block in range(user_blocks)
            ],
            axis=0,
        ).astype(jnp.float32)
        weighted = (scores * w).astype(jnp.bfloat16)
        total = jnp.dot(weighted, factors, preferred_element_type=jnp.float32)
        if phase == 0:
            targets = jnp.where(w > 0, w + 1.0, 0.0).astype(jnp.bfloat16)
            total = jnp.dot(targets, factors, preferred_element_type=jnp.float32) - total
        part[phase] += total
        if phase == 0:
            gram[...] += lax.dot_general(
                factors, factors, (((0,), (0,)), ((), ())), preferred_element_type=jnp.float32
            )

    def first_pass(offset):
        base = flip(col, offset) * own_blocks

        def body(i, carry):
            terms(0, base + i * WIDE)
            return carry

        lax.fori_loop(0, own_blocks // WIDE, body, 0)

    evens = [m for m in range(2, n_col, 2)]
    early = [m for m in evens if m in singles]
    late = [m for m in evens if m not in singles]
    first_pass(0)
    for place, m in enumerate(early):
        receive(m, place % HALVES)
    for half in range(HALVES):
        receive(1, half)
    first_pass(1)
    for place, m in enumerate(early):
        receive(m, (place + 1) % HALVES)
    for m in early:
        first_pass(m)
    for m in late:
        for half in range(HALVES):
            receive(m, half)
    for m in early:
        for half in range(HALVES):
            receive(m + 1, half)
        first_pass(m + 1)
    for m in late:
        first_pass(m)
    for m in late:
        for half in range(HALVES):
            receive(m + 1, half)
        first_pass(m + 1)

    part[0] -= jnp.dot(
        start_users[...].reshape(part.shape[1:]), gram[...], precision=lax.Precision.HIGHEST,
        preferred_element_type=jnp.float32,
    )
    for d in peers:
        sum_copy(0, d).start()
    for d in peers:
        gram_copy(d).start()
    residual = part[0, own, :] - RIDGE * user_ref[...]
    for d in peers:
        sum_copy(0, d).wait_recv()
    for d in peers:
        residual += inbox[0, d - 1]
    resid_ref[...] = residual
    direction[...] = residual
    norm_now = jnp.sum(residual * residual, axis=1, keepdims=True)

    for step in range(ITERS):
        users[step + 1, row] = direction[...].astype(jnp.bfloat16)
        for d in peers:
            users_copy(step, d).start()
        for d in peers:
            users_copy(step, d).wait_recv()

        def body(i, carry, phase=step + 1):
            terms(phase, i * WIDE)
            return carry

        lax.fori_loop(0, item_blocks // WIDE, body, 0)
        for d in peers:
            sum_copy(step + 1, d).start()
        if step == 0:
            for d in peers:
                gram_copy(d).wait()
            whole = gram[...]
            for d in peers:
                whole += gram_in[d - 1]
            gram[...] = whole
        vector = direction[...]
        image = (
            jnp.dot(
                vector, gram[...], precision=lax.Precision.HIGHEST,
                preferred_element_type=jnp.float32,
            )
            + RIDGE * vector
            + part[step + 1, own, :]
        )
        for d in peers:
            sum_copy(step + 1, d).wait_recv()
        for d in peers:
            image += inbox[step + 1, d - 1]
        step_size = norm_now / (jnp.sum(vector * image, axis=1, keepdims=True) + EPSILON)
        spread = jnp.broadcast_to(step_size, (size, size))
        steps[step, row] = spread.T[:8]
        for d in peers:
            steps_copy(step, d).start()
        residual = resid_ref[...] - step_size * image
        resid_ref[...] = residual
        norm_next = jnp.sum(residual * residual, axis=1, keepdims=True)
        direction[...] = residual + norm_next / (norm_now + EPSILON) * vector
        norm_now = norm_next

    for step in range(ITERS):
        for d in peers:
            steps_copy(step, d).wait_recv()
    source = slot_ref[0, 0]
    answer = start_users[source]
    for step in range(ITERS):
        scale = jnp.broadcast_to(steps[step, source][0:1], (size, size)).T
        answer += scale * users[step + 1, source].astype(jnp.float32)
    solved_ref[...] = answer

    for m, h in pending:
        gather_copy(m, h).wait_send()
    for d in peers:
        start_copy(d).wait_send()
        for phase in range(ITERS + 1):
            sum_copy(phase, d).wait_send()
        for step in range(ITERS):
            users_copy(step, d).wait_send()
            steps_copy(step, d).wait_send()


def local(n_row, n_col, user_factors, item_factors, confidence, tile_coords, relay_source):
    size = confidence.shape[-1]
    width = item_factors.shape[1]
    tiles = tile_coords.shape[2]
    group_items = item_factors.shape[0] * n_col
    item_blocks = group_items // size
    group_users = user_factors.shape[0] * n_row
    coords = tile_coords[0, 0]
    key = coords[:, 0] * item_blocks + coords[:, 1]
    places = jnp.arange(n_row * item_blocks, dtype=jnp.int32)
    number = jnp.arange(tiles, dtype=jnp.int32)
    where = jnp.min(
        jnp.where(key[None, :] == places[:, None], number[None, :], tiles), axis=1
    ).astype(jnp.int32)
    kinds = 3 + 3 * ITERS
    vmem = pl.BlockSpec(memory_space=pltpu.VMEM)
    smem = pl.BlockSpec(memory_space=pltpu.SMEM)
    outs = jax.ShapeDtypeStruct(user_factors.shape, jnp.float32)
    return pl.pallas_call(
        functools.partial(kernel, n_row, n_col, size),
        out_shape=(outs, outs),
        in_specs=[smem, smem, vmem, vmem, pl.BlockSpec(memory_space=pl.ANY)],
        out_specs=(vmem, vmem),
        scratch_shapes=[
            pltpu.VMEM((tiles + 1, size, size), jnp.bfloat16),
            pltpu.VMEM((group_items, width), jnp.bfloat16),
            pltpu.VMEM((n_row, size, width), jnp.float32),
            pltpu.VMEM((ITERS + 1, n_row, size, width), jnp.bfloat16),
            pltpu.VMEM((ITERS + 1, group_users, width), jnp.float32),
            pltpu.VMEM((ITERS + 1, n_row - 1, size, width), jnp.float32),
            pltpu.VMEM((width, width), jnp.float32),
            pltpu.VMEM((n_row - 1, width, width), jnp.float32),
            pltpu.VMEM((ITERS, n_row, 8, size), jnp.float32),
            pltpu.VMEM((size, width), jnp.float32),
            pltpu.SemaphoreType.DMA,
            pltpu.SemaphoreType.DMA,
            pltpu.SemaphoreType.DMA((n_col, HALVES)),
            pltpu.SemaphoreType.DMA((n_col, HALVES)),
            pltpu.SemaphoreType.DMA((kinds, n_row)),
            pltpu.SemaphoreType.DMA((kinds, n_row)),
        ],
        compiler_params=pltpu.CompilerParams(
            collective_id=0, has_side_effects=True, vmem_limit_bytes=48 * 2**20
        ),
    )(where, relay_source, user_factors, item_factors, confidence.reshape(tiles, size, size))


def solution(mesh):
    return jax.shard_map(
        functools.partial(local, mesh.shape["row"], mesh.shape["col"]),
        mesh=mesh,
        in_specs=(
            P(("col", "row"), None),
            P(("row", "col"), None),
            P("row", "col", None, None),
            P("row", "col", None, None),
            P("col", "row"),
        ),
        out_specs=(P(("col", "row"), None), P(("col", "row"), None)),
        check_vma=False,
    )
```
